32 devices in a mesh: gy: 4 (over y, core), gx: 8 (over z, x).
Axes of the slice: x: 2, y: 2, z: 4, core: 2. Of those that a mesh axis runs over, the one named last changes fastest.
Arguments:
- concentration: float32 [32, 1024, 1024], P('gx', None, 'gy'), may hold values from -3 to 3
Outputs:
- increment: float32 [32, 1024, 1024], P('gx', None, 'gy')
The draws below stay inside these ranges and needn't reach their ends.
All inputs are finite; a program needn't handle non-finite values.
Results may differ from the reference program's by a relative error of at most 0.0003.
Values sent between devices are 32-bit elements; how exact they have to be, the bound alone decides.
A program may use at most 64 MiB of HBM per device.

```python
import jax
import jax.numpy as jnp
from jax import lax

NX = 1024
NY = 1024
NZ = 32


def levels(own_key, dims, cuts, low, largest):
    level = 1.0
    for dim, blocks in cuts:
        heights = jax.random.uniform(jax.random.fold_in(jax.random.fold_in(own_key, 6), dim), (blocks,), jnp.float32, low / len(cuts), largest / len(cuts))
        level = level * jnp.repeat(jnp.exp(heights), dims[dim] // blocks).reshape((-1,) + (1,) * (len(dims) - 1 - dim))
    return level


def normal_values(own_key, extent, scale, bound, shards=(), held_as=jnp.bfloat16):
    entries = scale * jax.random.normal(own_key, extent, jnp.float32)
    if shards:
        entries = entries * levels(own_key, extent, shards, -0.22, 0.18)
    return jnp.clip(entries, -bound, bound).astype(held_as)


def setup_inputs(seed: int = 0) -> dict:
    streams_of = jax.random.split(jax.random.key(seed), 2)
    concentration = normal_values(streams_of[0], (NZ, NX, NY), 0.5, 3.0, ((0, 8), (2, 4)), jnp.float32)
    return dict(concentration=concentration)


STRENGTH = 16.0
STEP = 2.0
HIGH = lax.Precision.HIGHEST

def laplace_inner(padded):
    total = padded[2:, 1:-1, 1:-1] + padded[:-2, 1:-1, 1:-1]
    total = total + padded[1:-1, 2:, 1:-1] + padded[1:-1, :-2, 1:-1]
    total = total + padded[1:-1, 1:-1, 2:] + padded[1:-1, 1:-1, :-2]
    return total - 6.0 * padded[1:-1, 1:-1, 1:-1]

def laplace(values):
    return laplace_inner(jnp.pad(values, 1))

def line_inverse(length, number_type):
    position = jnp.arange(length)
    distance = jnp.abs(position[:, None] - position[None, :])
    banded = jnp.where(distance == 0, 6.0, jnp.where(distance == 1, -4.0, jnp.where(distance == 2, 1.0, 0.0)))
    matrix = jnp.eye(length, dtype=number_type) + STRENGTH * banded.astype(number_type)
    return jnp.linalg.solve(matrix, jnp.eye(length, dtype=number_type))

def apply_along(values, length, dimension):
    inverse = line_inverse(length, values.dtype)
    rotated = jnp.tensordot(inverse, values, axes=([1], [dimension]), precision=HIGH)
    return jnp.moveaxis(rotated, 0, dimension)

def reference(concentration):
    conc = concentration
    potential = conc * conc * conc - conc - laplace(conc)
    source = STEP * laplace(potential)
    after_x = apply_along(source, NX, 1)
    after_y = apply_along(after_x, NY, 2)
    return apply_along(after_y, NZ, 0)
```

```python
import functools

import jax
import jax.numpy as jnp
import numpy as np
from jax import lax
from jax.experimental import pallas as pl
from jax.experimental.pallas import tpu as pltpu
from jax.sharding import PartitionSpec as P

STRENGTH = 16.0
STEP = 2.0
HALO = 2
CHUNKS = 2
FINE = lax.Precision.HIGHEST


def banded(length):
    eye = functools.partial(np.eye, length)
    stencil = 6.0 * eye() - 4.0 * (eye(k=1) + eye(k=-1)) + eye(k=2) + eye(k=-2)
    return eye() + STRENGTH * stencil


def coupling():
    return STRENGTH * np.array([[1.0, 0.0], [-4.0, 1.0]])


def split_line_maps(length, blocks):
    span = length // blocks
    local = np.linalg.inv(banded(span))
    cross = coupling()
    rows = np.array([0, 1, span - 2, span - 1])
    feed = np.zeros((blocks, span, 4 * blocks))
    for block in range(blocks):
        if block > 0:
            feed[block][:, 4 * block - 2 : 4 * block] = local[:, :2] @ cross.T
        if block < blocks - 1:
            feed[block][:, 4 * block + 4 : 4 * block + 6] = local[:, -2:] @ cross
    system = np.eye(4 * blocks) + np.concatenate([feed[b][rows] for b in range(blocks)])
    correct = feed @ np.linalg.inv(system)
    as32 = lambda a: np.ascontiguousarray(a, dtype=np.float32)
    return as32(local), as32(local[rows]), as32(correct)


def two_ended_maps(length, groups):
    span = length // groups
    half = groups // 2
    cross = coupling()
    inner = np.zeros((span, 2))
    inner[-2:] = cross
    outer = np.zeros((span, 2))
    outer[:2] = cross.T
    edge_maps, full_maps = [], []
    corner = np.zeros((2, 2))
    inverses = []
    for depth in range(half):
        schur = banded(span)
        schur[:2, :2] -= cross.T @ corner @ cross
        inverse = np.linalg.inv(schur)
        inverses.append(inverse)
        corner = inverse[-2:, -2:]
        reach = outer if depth > 0 else np.zeros_like(outer)
        edge_maps.append(np.concatenate([inverse, -inverse @ reach], axis=1))
    for depth in range(half):
        known = edge_maps[depth]
        back = inverses[depth] @ inner
        if depth < half - 1:
            full_maps.append(np.concatenate([known, -back], axis=1))
        else:
            swap = np.eye(2)[::-1]
            hold = back[-2:]
            far = swap @ hold @ swap
            joint = np.linalg.inv(np.eye(2) - far @ hold)
            own = known - back @ joint @ (-far) @ known[-2:]
            full_maps.append(np.concatenate([own, -back @ joint], axis=1))
    flip = np.arange(span)[::-1]
    two = np.array([1, 0])
    edges, outs, fulls = [], [], []
    for group in range(groups):
        mirrored = group >= half
        depth = groups - 1 - group if mirrored else group
        edge, full = edge_maps[depth][-2:], full_maps[depth]
        if mirrored:
            columns = np.concatenate([flip, span + two, span + 2 + two])
            edge = edge[two][:, columns[: span + 2]]
            full = full[flip][:, columns]
            out = full[-2:]
        else:
            out = full[:2]
        edges.append(edge)
        outs.append(out)
        fulls.append(full)
    stack = lambda a: np.ascontiguousarray(np.stack(a), dtype=np.float32)
    return stack(edges), stack(outs), stack(fulls)


def mix_kernel(counts, matrix_ref, *refs):
    out_ref = refs[-1]
    inputs = refs[:-1]
    for row in range(out_ref.shape[0]):
        total, column = None, 0
        for ref, count in zip(inputs, counts):
            for plane in range(count):
                term = matrix_ref[row, column] * ref[plane]
                total = term if total is None else total + term
                column += 1
        out_ref[row] = total


def mix(matrix, *arrays):
    counts = tuple(a.shape[0] for a in arrays)
    rows, width = arrays[0].shape[1:]
    tile = 32
    spec = lambda planes: pl.BlockSpec((planes, tile, width), lambda i: (0, i, 0))
    total = sum(counts) + matrix.shape[0]
    return pl.pallas_call(
        functools.partial(mix_kernel, counts),
        grid=(rows // tile,),
        in_specs=[pl.BlockSpec(memory_space=pltpu.SMEM)] + [spec(c) for c in counts],
        out_specs=spec(matrix.shape[0]),
        out_shape=jax.ShapeDtypeStruct((matrix.shape[0], rows, width), jnp.float32),
        cost_estimate=pl.CostEstimate(
            flops=2 * matrix.shape[0] * sum(counts) * rows * width,
            bytes_accessed=4 * total * rows * width,
            transcendentals=0,
        ),
    )(matrix, *arrays)


def laplace_inner(padded):
    total = padded[2:, 1:-1, 1:-1] + padded[:-2, 1:-1, 1:-1]
    total = total + padded[1:-1, 2:, 1:-1] + padded[1:-1, :-2, 1:-1]
    total = total + padded[1:-1, 1:-1, 2:] + padded[1:-1, 1:-1, :-2]
    return total - 6.0 * padded[1:-1, 1:-1, 1:-1]


def pick(table, index):
    return lax.dynamic_index_in_dim(jnp.asarray(table), index, 0, keepdims=False)


def pad_x(values):
    return jnp.pad(values, ((0, 0), (1, 1), (0, 0)))


def body(concentration):
    planes, cells_x, cells_y = concentration.shape
    count, blocks = lax.axis_size("gx"), lax.axis_size("gy")
    groups, half_x = count // 2, cells_x // 2
    rank, rank_y = lax.axis_index("gx"), lax.axis_index("gy")
    side, group = rank % 2, rank // 2
    first = side == 0
    rows = half_x + 8
    partner = [(i, i ^ 1) for i in range(count)]
    up = [(i, i + 2) for i in range(count - 2)]
    down = [(b, a) for a, b in up]

    own = lax.dynamic_slice_in_dim(concentration, side * (cells_x - rows), rows, 1)
    give = lax.dynamic_slice_in_dim(concentration, (1 - side) * (cells_x - rows), rows, 1)
    got = lax.ppermute(give, "gx", partner)
    low, high = jnp.where(first, own, got), jnp.where(first, got, own)
    below = lax.ppermute(high[-HALO:], "gx", up)
    above = lax.ppermute(low[:HALO], "gx", down)
    block = jnp.concatenate([below, low, high, above], axis=0)
    right = [(i, i + 1) for i in range(blocks - 1)]
    left = [(b, a) for a, b in right]
    columns = lambda v: jnp.moveaxis(v, 2, 0)
    before = lax.ppermute(columns(block[:, :, -HALO:]), "gy", right)
    behind = lax.ppermute(columns(block[:, :, :HALO]), "gy", left)
    wide = jnp.concatenate(
        [jnp.moveaxis(before, 0, 2), block, jnp.moveaxis(behind, 0, 2)], axis=2
    )
    centre = wide[1:-1, :, 1:-1]
    potential = centre * centre * centre - centre - laplace_inner(pad_x(wide))
    layer = lax.broadcasted_iota(jnp.int32, potential.shape, 0)
    column = lax.broadcasted_iota(jnp.int32, potential.shape, 2)
    outside = (layer == 0) & (group == 0)
    outside |= (layer == potential.shape[0] - 1) & (group == groups - 1)
    outside |= (column == 0) & (rank_y == 0)
    outside |= (column == cells_y + 1) & (rank_y == blocks - 1)
    potential = jnp.where(outside, 0.0, potential)
    source = STEP * laplace_inner(pad_x(potential))
    source = lax.dynamic_slice_in_dim(source, side * 8, half_x, 1)

    edge_map, out_map, full_map = two_ended_maps(planes * count, groups)
    edge_map, out_map, full_map = (pick(t, group) for t in (edge_map, out_map, full_map))
    middle = groups // 2
    def hop(values, sends):
        return lax.ppermute(
            values, "gx", [(2 * a + s, 2 * b + s) for a, b in sends for s in range(2)]
        )
    inward = [
        [(d, d + 1), (groups - 1 - d, groups - 2 - d)] for d in range(middle - 1)
    ]
    chunk = half_x // CHUNKS
    pieces = []
    for part in range(CHUNKS):
        piece = source[:, part * chunk : (part + 1) * chunk]
        outer = jnp.zeros((2, chunk, cells_y), jnp.float32)
        for step, sends in enumerate(inward):
            if step == 0:
                edge = mix(edge_map[:, : 2 * planes], piece)
                outer = hop(edge, sends)
            else:
                outer = outer + hop(mix(edge_map, piece, outer), sends)
        inner = hop(
            mix(edge_map, piece, outer), [(middle - 1, middle), (middle, middle - 1)]
        )
        for sends in reversed(inward):
            inner = inner + hop(mix(out_map, piece, outer, inner), [(b, a) for a, b in sends])
        solved = mix(full_map, piece, outer, inner)
        keep = jnp.where(first, solved[:planes], solved[planes:])
        send = jnp.where(first, solved[planes:], solved[:planes])
        back = lax.ppermute(send, "gx", partner)
        pieces.append((jnp.where(first, keep, back), jnp.where(first, back, keep)))
    after_z = jnp.concatenate([p[0] for p in pieces] + [p[1] for p in pieces], axis=1)

    local, edge_rows, correct = split_line_maps(cells_y * blocks, blocks)
    edges = jnp.einsum("ij,axj->iax", edge_rows, after_z, precision=FINE)
    edges = edges.reshape(4, planes * cells_x)
    everyone = lax.all_gather(edges, "gy", axis=0, tiled=True)
    everyone = everyone.reshape(4 * blocks, planes, cells_x)
    after_y = jnp.einsum("axj,ji->axi", after_z, local, precision=FINE)
    after_y = after_y - jnp.einsum("qax,iq->axi", everyone, pick(correct, rank_y), precision=FINE)

    inverse_x = np.ascontiguousarray(np.linalg.inv(banded(cells_x)), dtype=np.float32)
    return jnp.einsum("ij,ajb->aib", inverse_x, after_y, precision=FINE)


def solution(mesh):
    return jax.shard_map(
        body,
        mesh=mesh,
        in_specs=(P("gx", None, "gy"),),
        out_specs=P("gx", None, "gy"),
        check_vma=False,
    )
```

```python
import functools

import jax
import jax.numpy as jnp
import numpy as np
from jax import lax
from jax.experimental import pallas as pl
from jax.experimental.pallas import tpu as pltpu
from jax.sharding import PartitionSpec as P

STRENGTH = 16.0
STEP = 2.0
HALO = 2
CHUNKS = 2
FINE = lax.Precision.HIGHEST


def banded(length):
    eye = functools.partial(np.eye, length)
    stencil = 6.0 * eye() - 4.0 * (eye(k=1) + eye(k=-1)) + eye(k=2) + eye(k=-2)
    return eye() + STRENGTH * stencil


def coupling():
    return STRENGTH * np.array([[1.0, 0.0], [-4.0, 1.0]])


def split_line_maps(length, blocks):
    span = length // blocks
    local = np.linalg.inv(banded(span))
    cross = coupling()
    rows = np.array([0, 1, span - 2, span - 1])
    feed = np.zeros((blocks, span, 4 * blocks))
    for block in range(blocks):
        if block > 0:
            feed[block][:, 4 * block - 2 : 4 * block] = local[:, :2] @ cross.T
        if block < blocks - 1:
            feed[block][:, 4 * block + 4 : 4 * block + 6] = local[:, -2:] @ cross
    system = np.eye(4 * blocks) + np.concatenate([feed[b][rows] for b in range(blocks)])
    correct = feed @ np.linalg.inv(system)
    as32 = lambda a: np.ascontiguousarray(a, dtype=np.float32)
    return as32(local), as32(local[rows]), as32(correct)


def two_ended_maps(length, groups):
    span = length // groups
    half = groups // 2
    cross = coupling()
    inner = np.zeros((span, 2))
    inner[-2:] = cross
    outer = np.zeros((span, 2))
    outer[:2] = cross.T
    edge_maps, full_maps = [], []
    corner = np.zeros((2, 2))
    inverses = []
    for depth in range(half):
        schur = banded(span)
        schur[:2, :2] -= cross.T @ corner @ cross
        inverse = np.linalg.inv(schur)
        inverses.append(inverse)
        corner = inverse[-2:, -2:]
        reach = outer if depth > 0 else np.zeros_like(outer)
        edge_maps.append(np.concatenate([inverse, -inverse @ reach], axis=1))
    for depth in range(half):
        known = edge_maps[depth]
        back = inverses[depth] @ inner
        if depth < half - 1:
            full_maps.append(np.concatenate([known, -back], axis=1))
        else:
            swap = np.eye(2)[::-1]
            hold = back[-2:]
            far = swap @ hold @ swap
            joint = np.linalg.inv(np.eye(2) - far @ hold)
            own = known - back @ joint @ (-far) @ known[-2:]
            full_maps.append(np.concatenate([own, -back @ joint], axis=1))
    flip = np.arange(span)[::-1]
    two = np.array([1, 0])
    edges, outs, fulls = [], [], []
    for group in range(groups):
        mirrored = group >= half
        depth = groups - 1 - group if mirrored else group
        edge, full = edge_maps[depth][-2:], full_maps[depth]
        if mirrored:
            columns = np.concatenate([flip, span + two, span + 2 + two])
            edge = edge[two][:, columns[: span + 2]]
            full = full[flip][:, columns]
            out = full[-2:]
        else:
            out = full[:2]
        edges.append(edge)
        outs.append(out)
        fulls.append(full)
    stack = lambda a: np.ascontiguousarray(np.stack(a), dtype=np.float32)
    return stack(edges), stack(outs), stack(fulls)


def mix_kernel(counts, matrix_ref, *refs):
    out_ref = refs[-1]
    inputs = refs[:-1]
    for row in range(out_ref.shape[0]):
        total, column = None, 0
        for ref, count in zip(inputs, counts):
            for plane in range(count):
                term = matrix_ref[row, column] * ref[plane]
                total = term if total is None else total + term
                column += 1
        out_ref[row] = total


def mix(matrix, *arrays):
    counts = tuple(a.shape[0] for a in arrays)
    rows, width = arrays[0].shape[1:]
    tile = min(rows, 128)
    spec = lambda planes: pl.BlockSpec((planes, tile, width), lambda i: (0, i, 0))
    total = sum(counts) + matrix.shape[0]
    return pl.pallas_call(
        functools.partial(mix_kernel, counts),
        grid=(rows // tile,),
        in_specs=[pl.BlockSpec(memory_space=pltpu.SMEM)] + [spec(c) for c in counts],
        out_specs=spec(matrix.shape[0]),
        out_shape=jax.ShapeDtypeStruct((matrix.shape[0], rows, width), jnp.float32),
        cost_estimate=pl.CostEstimate(
            flops=2 * matrix.shape[0] * sum(counts) * rows * width,
            bytes_accessed=4 * total * rows * width,
            transcendentals=0,
        ),
    )(matrix, *arrays)


def stencil_kernel(place_ref, wide_ref, out_ref, potential, whole):
    planes, rows, width = wide_ref.shape
    cells_y = out_ref.shape[2]
    row = lax.broadcasted_iota(jnp.int32, (rows, width), 0)
    column = lax.broadcasted_iota(jnp.int32, (rows, width), 1)

    def laplace(ref, plane):
        centre = ref[plane]
        total = ref[plane - 1] + ref[plane + 1] - 6.0 * centre
        total = total + jnp.where(row == 0, 0.0, pltpu.roll(centre, 1, 0))
        total = total + jnp.where(row == rows - 1, 0.0, pltpu.roll(centre, rows - 1, 0))
        return centre, total + pltpu.roll(centre, 1, 1) + pltpu.roll(centre, width - 1, 1)

    @pl.loop(1, planes - 1)
    def _(plane):
        centre, around = laplace(wide_ref, plane)
        value = centre * centre * centre - centre - around
        hidden = (column == width - 1) & (place_ref[2] == 1)
        hidden = hidden | ((column == cells_y) & (place_ref[3] == 1))
        potential[plane - 1] = jnp.where(hidden, 0.0, value)

    @pl.when(place_ref[0] == 1)
    def _():
        potential[0] = jnp.zeros((rows, width), jnp.float32)

    @pl.when(place_ref[1] == 1)
    def _():
        potential[planes - 3] = jnp.zeros((rows, width), jnp.float32)

    start = pl.multiple_of(place_ref[4] * 8, 8)

    @pl.loop(1, planes - 3)
    def _(plane):
        whole[...] = STEP * laplace(potential, plane)[1]
        out_ref[plane - 1] = whole[pl.ds(start, out_ref.shape[1]), :cells_y]


def stencil(place, wide, cells_y):
    planes, rows, width = wide.shape
    vmem = pl.BlockSpec(memory_space=pltpu.VMEM)
    return pl.pallas_call(
        stencil_kernel,
        in_specs=[pl.BlockSpec(memory_space=pltpu.SMEM), vmem],
        out_specs=vmem,
        out_shape=jax.ShapeDtypeStruct((planes - 4, rows - 8, cells_y), jnp.float32),
        scratch_shapes=[
            pltpu.VMEM((planes - 2, rows, width), jnp.float32),
            pltpu.VMEM((rows, width), jnp.float32),
        ],
        compiler_params=pltpu.CompilerParams(vmem_limit_bytes=44 * 2**20),
    )(place, wide)


def pick(table, index):
    return lax.dynamic_index_in_dim(jnp.asarray(table), index, 0, keepdims=False)


def body(concentration):
    planes, cells_x, cells_y = concentration.shape
    count, blocks = lax.axis_size("gx"), lax.axis_size("gy")
    groups, half_x = count // 2, cells_x // 2
    rank, rank_y = lax.axis_index("gx"), lax.axis_index("gy")
    side, group = rank % 2, rank // 2
    first = side == 0
    rows = half_x + 8
    partner = [(i, i ^ 1) for i in range(count)]
    up = [(i, i + 2) for i in range(count - 2)]
    down = [(b, a) for a, b in up]

    own = lax.dynamic_slice_in_dim(concentration, side * (cells_x - rows), rows, 1)
    give = lax.dynamic_slice_in_dim(concentration, (1 - side) * (cells_x - rows), rows, 1)
    got = lax.ppermute(give, "gx", partner)
    low, high = jnp.where(first, own, got), jnp.where(first, got, own)
    below = lax.ppermute(high[-HALO:], "gx", up)
    above = lax.ppermute(low[:HALO], "gx", down)
    block = jnp.concatenate([below, low, high, above], axis=0)
    right = [(i, i + 1) for i in range(blocks - 1)]
    left = [(b, a) for a, b in right]
    columns = lambda v: jnp.moveaxis(v, 2, 0)
    before = lax.ppermute(columns(block[:, :, -HALO:]), "gy", right)
    behind = lax.ppermute(columns(block[:, :, :HALO]), "gy", left)
    filler = jnp.zeros(block.shape[:2] + (128 - 2 * HALO,), jnp.float32)
    wide = jnp.concatenate(
        [block, jnp.moveaxis(behind, 0, 2), filler, jnp.moveaxis(before, 0, 2)], axis=2
    )
    place = [group == 0, group == groups - 1, rank_y == 0, rank_y == blocks - 1, side == 1]
    source = stencil(jnp.stack(place).astype(jnp.int32), wide, cells_y)

    edge_map, out_map, full_map = two_ended_maps(planes * count, groups)
    edge_map, out_map, full_map = (pick(t, group) for t in (edge_map, out_map, full_map))
    middle = groups // 2
    def hop(values, sends):
        return lax.ppermute(
            values, "gx", [(2 * a + s, 2 * b + s) for a, b in sends for s in range(2)]
        )
    inward = [
        [(d, d + 1), (groups - 1 - d, groups - 2 - d)] for d in range(middle - 1)
    ]
    chunk = half_x // CHUNKS
    pieces = []
    for part in range(CHUNKS):
        piece = source[:, part * chunk : (part + 1) * chunk]
        outer = jnp.zeros((2, chunk, cells_y), jnp.float32)
        for step, sends in enumerate(inward):
            if step == 0:
                edge = mix(edge_map[:, : 2 * planes], piece)
                outer = hop(edge, sends)
            else:
                outer = outer + hop(mix(edge_map, piece, outer), sends)
        inner = hop(
            mix(edge_map, piece, outer), [(middle - 1, middle), (middle, middle - 1)]
        )
        for sends in reversed(inward):
            inner = inner + hop(mix(out_map, piece, outer, inner), [(b, a) for a, b in sends])
        solved = mix(full_map, piece, outer, inner)
        keep = jnp.where(first, solved[:planes], solved[planes:])
        send = jnp.where(first, solved[planes:], solved[:planes])
        back = lax.ppermute(send, "gx", partner)
        pieces.append((jnp.where(first, keep, back), jnp.where(first, back, keep)))
    after_z = jnp.concatenate([p[0] for p in pieces] + [p[1] for p in pieces], axis=1)

    local, edge_rows, correct = split_line_maps(cells_y * blocks, blocks)
    edges = jnp.einsum("ij,axj->iax", edge_rows, after_z, precision=FINE)
    edges = edges.reshape(4, planes * cells_x)
    everyone = lax.all_gather(edges, "gy", axis=0, tiled=True)
    everyone = everyone.reshape(4 * blocks, planes, cells_x)
    after_y = jnp.einsum("axj,ji->axi", after_z, local, precision=FINE)
    after_y = after_y - jnp.einsum("qax,iq->axi", everyone, pick(correct, rank_y), precision=FINE)

    inverse_x = np.ascontiguousarray(np.linalg.inv(banded(cells_x)), dtype=np.float32)
    return jnp.einsum("ij,ajb->aib", inverse_x, after_y, precision=FINE)


def solution(mesh):
    return jax.shard_map(
        body,
        mesh=mesh,
        in_specs=(P("gx", None, "gy"),),
        out_specs=P("gx", None, "gy"),
        check_vma=False,
    )
```
